1024 devices in a mesh: blk: 64 (over z, y_lo), grp: 16 (over x, y_hi, core).
Axes of the slice: x: 4, y: 4 (y_hi: 2, y_lo: 2; y = y_hi * 2 + y_lo), z: 32, core: 2. Of those that a mesh axis runs over, the one named last changes fastest.
Arguments:
- image: bfloat16 [49152, 1152], P(('blk', 'grp')), may hold values from -0.1796875 to 0.1796875
- text: bfloat16 [49152, 1152], P(('blk', 'grp')), may hold values from -0.1796875 to 0.1796875
- log_scale: float32 [1], replicated, may hold values from 0 to 1.1
- bias: float32 [1], replicated, may hold values from -2 to 0
Outputs:
- loss_rows: float32 [49152], P(('blk', 'grp'))
- grad_image: float32 [49152, 1152], P(('blk', 'grp'))
- grad_text: float32 [49152, 1152], P(('blk', 'grp'))
The draws below stay inside these ranges and needn't reach their ends.
All inputs are finite; a program needn't handle non-finite values.
Results may differ from the reference program's by a relative error of at most 0.0044.
Values may be sent and summed in bfloat16 or wider, within the bound.
No kernel may reach another device: no remote copies, remote signals or barrier semaphores. Data moves between devices by JAX's collectives and lax.ppermute only.
A program may use at most 32 MiB of HBM per device.

```python
import jax
import jax.numpy as jnp
from jax import lax

D = 1152
R = 48
STEPS = 8
B = 49152
N_BLK = 64
N_GRP = 16


def block_levels(stream_key, dims, split, smallest, high):
    factor_of, own = 1.0, jax.random.fold_in(stream_key, 6)
    for dim, parts in split:
        steps = jnp.exp(jax.random.uniform(jax.random.fold_in(own, dim), (parts,), jnp.float32, smallest / len(split), high / len(split)))
        factor_of = factor_of * jnp.repeat(steps, dims[dim] // parts).reshape([-1 if axis == dim else 1 for axis in range(len(dims))])
    return factor_of


def bell_draw(own_key, extent, scale, reach, split=(), kind=jnp.bfloat16):
    level = block_levels(own_key, extent, split, -0.22, 0.18) if split else 1.0
    array = jax.random.normal(own_key, extent, jnp.float32) * scale * level
    return jnp.minimum(jnp.maximum(array, -reach), reach).astype(kind)


def setup_inputs(seed: int = 0) -> dict:
    keys = jax.random.split(jax.random.key(seed), 5)
    return {
        "image": bell_draw(keys[0], (B, D), 0.03, 0.1796875, ((0, 1024),)),
        "text": bell_draw(keys[1], (B, D), 0.03, 0.1796875, ((0, 1024),)),
        "log_scale": jnp.clip(jax.random.uniform(keys[2], (1,), jnp.float32, 0.0, 1.1), 0.0, 1.1),
        "bias": jnp.clip(jax.random.uniform(keys[3], (1,), jnp.float32, -2.0, 0.0), -2.0, 0.0),
    }


EPS = 1e-06

def normed(rows):
    values = rows.astype(jnp.float32)
    norm = jnp.sqrt(lax.optimization_barrier(jnp.sum(values * values, axis=-1, keepdims=True)) + EPS)
    return (values / norm, norm)

def project(unit_grad, unit, norm):
    inner = lax.optimization_barrier(jnp.sum(unit * unit_grad, axis=-1, keepdims=True))
    return (unit_grad - unit * inner) / norm

def reference(image, text, log_scale, bias):
    group_rows = R * N_GRP
    image_unit, image_norm = normed(image)
    text_unit, text_norm = normed(text)
    image_low = lax.optimization_barrier(image_unit.astype(jnp.bfloat16))
    text_low = lax.optimization_barrier(text_unit.astype(jnp.bfloat16))
    image_blocks = image_low.astype(jnp.float32).reshape(N_BLK, group_rows, D)
    text_blocks_own = text_low.astype(jnp.float32).reshape(N_BLK, group_rows, D)
    scale_factor = jnp.exp(log_scale[0])
    shift_bias = bias[0]
    identity = jnp.eye(group_rows, dtype=jnp.float32)
    unit_grad_image = jnp.zeros((N_BLK, group_rows, D), jnp.float32)
    unit_grad_text = jnp.zeros((N_BLK, group_rows, D), jnp.float32)
    loss_sum = jnp.zeros((N_BLK, group_rows), jnp.float32)
    for offset in range(STEPS):
        text_blocks = jnp.roll(text_blocks_own, -offset, axis=0)
        logit = scale_factor * jnp.einsum('bid,bjd->bij', image_blocks, text_blocks) + shift_bias
        positive = identity if offset == 0 else jnp.zeros_like(identity)
        term = jax.nn.softplus(logit) - positive * logit
        coef = lax.optimization_barrier((jax.nn.sigmoid(logit) - positive).astype(jnp.bfloat16)).astype(jnp.float32)
        loss_sum = loss_sum + lax.optimization_barrier(jnp.sum(term, axis=2))
        unit_grad_image = unit_grad_image + scale_factor * jnp.einsum('bij,bjd->bid', coef, text_blocks)
        text_term = scale_factor * jnp.einsum('bij,bid->bjd', coef, image_blocks)
        unit_grad_text = unit_grad_text + jnp.roll(text_term, offset, axis=0)
    loss_rows = loss_sum.reshape(B) / (STEPS * group_rows)
    grad_image = project(unit_grad_image.reshape(B, D), image_unit, image_norm)
    grad_text = project(unit_grad_text.reshape(B, D), text_unit, text_norm)
    return (loss_rows, grad_image, grad_text)
```

```python
import functools

import jax
import jax.numpy as jnp
from jax import lax
from jax.experimental import pallas as pl
from jax.experimental.pallas import tpu as pltpu
from jax.sharding import PartitionSpec as P

STEPS = 8
EPS = 1e-06
PLANE = ("yl", "x", "yh")
SLOTS = 5
TEXT_ROWS = 256
EXTRA = 128
LIMIT = 48 * 1024 * 1024


def call(kernel, out_shape, **kwargs):
    return pl.pallas_call(
        kernel,
        out_shape=out_shape,
        compiler_params=pltpu.CompilerParams(vmem_limit_bytes=LIMIT),
        **kwargs,
    )


def to_behind(value, slot):
    planes = lax.axis_size("z")
    parities = (0, 1) if slot < SLOTS - 1 else (0,)
    pairs = [(2 * z + yl, 2 * ((z - slot) % planes) + yl) for z in range(planes) for yl in parities]
    return lax.ppermute(value, ("z", "yl"), pairs)


def to_owner(value, slot):
    planes = lax.axis_size("z")
    parities = (0, 1) if slot < SLOTS - 1 else (0,)
    pairs = [(2 * z + yl, 2 * ((z + slot) % planes) + yl) for z in range(planes) for yl in parities]
    return lax.ppermute(value, ("z", "yl"), pairs)


def after(values, others):
    count = len(values)
    anywhere = pl.BlockSpec(memory_space=pl.ANY)
    return pl.pallas_call(
        lambda *refs: None,
        out_shape=tuple(jax.ShapeDtypeStruct(value.shape, value.dtype) for value in values),
        in_specs=[anywhere] * (count + len(others)),
        out_specs=(anywhere,) * count,
        input_output_aliases={i: i for i in range(count)},
    )(*values, *others)


def normed(rows):
    values = rows.astype(jnp.float32)
    norm = jnp.sqrt(jnp.sum(values * values, axis=-1, keepdims=True) + EPS)
    return (values / norm, norm)


def project(unit_grad, unit, norm):
    inner = jnp.sum(unit * unit_grad, axis=-1, keepdims=True)
    return (unit_grad - unit * inner) / norm


def prepare(image_ref, text_ref, image_low_ref, text_low_ref):
    image_low_ref[...] = normed(image_ref[...])[0].astype(jnp.bfloat16)
    text_low_ref[...] = normed(text_ref[...])[0].astype(jnp.bfloat16)


def score(log_scale_ref, bias_ref, place_ref, *refs):
    images = refs[0:2]
    texts = refs[2 : 2 + SLOTS]
    image_grads = refs[2 + SLOTS : 4 + SLOTS]
    text_grads = refs[4 + SLOTS : 4 + 2 * SLOTS]
    text_all, coef_all = refs[4 + 2 * SLOTS :]
    rows, width = texts[0].shape
    half = images[0].shape[0]
    block = half // 2
    for k in range(SLOTS):
        text_all[k * rows : (k + 1) * rows, :] = texts[k][...]
    text_all[SLOTS * rows :, :] = jnp.zeros((TEXT_ROWS - SLOTS * rows, width), jnp.bfloat16)
    scale = jnp.exp(jnp.full((1, 1), log_scale_ref[0], jnp.float32))
    parity, place = place_ref[0], place_ref[1]
    text = text_all[...]
    cols = lax.broadcasted_iota(jnp.int32, (1, TEXT_ROWS), 1)
    slot = jnp.zeros((1, TEXT_ROWS), jnp.int32)
    for k in range(1, SLOTS):
        slot = slot + (cols >= k * rows).astype(jnp.int32)
    lane = lax.broadcasted_iota(jnp.int32, (block, EXTRA), 1)
    row_ids = lax.broadcasted_iota(jnp.int32, (block, TEXT_ROWS), 0)
    col_ids = lax.broadcasted_iota(jnp.int32, (block, TEXT_ROWS), 1)
    for side in range(2):
        for own in range(2):
            here = slice(own * block, (own + 1) * block)
            logit = scale * lax.dot_general(
                images[side][here, :], text, (((1,), (1,)), ((), ())), preferred_element_type=jnp.float32
            ) + bias_ref[0]
            offset = 2 * slot + parity - own
            scored = ((offset >= 0) & (offset < STEPS) & (cols < SLOTS * rows)).astype(jnp.float32)
            grown = jnp.exp(logit)
            total = 1.0 + grown
            term = jnp.log(total)
            coef = grown / total
            if side == 0:
                positive = (row_ids == col_ids + place) & (col_ids < rows) & (parity == own)
                term = term - jnp.where(positive, logit, 0.0)
                coef = coef - jnp.where(positive, 1.0, 0.0)
            loss = jnp.sum(term * scored, axis=1, keepdims=True)
            loss_high = loss.astype(jnp.bfloat16).astype(jnp.float32)
            extra = jnp.where(lane == 0, loss_high, jnp.where(lane == 1, loss - loss_high, 0.0))
            coef = (coef * scored).astype(jnp.bfloat16)
            coef_all[side * half + own * block : side * half + (own + 1) * block, :] = coef
            image_grads[side][here, :width] = jnp.dot(
                coef, text, preferred_element_type=jnp.float32
            ).astype(jnp.bfloat16)
            image_grads[side][here, width:] = extra.astype(jnp.bfloat16)
    text_grad = lax.dot_general(
        coef_all[:half, :], images[0][...], (((0,), (0,)), ((), ())), preferred_element_type=jnp.float32
    ) + lax.dot_general(
        coef_all[half:, :], images[1][...], (((0,), (0,)), ((), ())), preferred_element_type=jnp.float32
    )
    for k in range(SLOTS):
        text_grads[k][...] = text_grad[k * rows : (k + 1) * rows, :].astype(jnp.bfloat16)


def add_pair(one_ref, two_ref, out_ref):
    out_ref[...] = (one_ref[...].astype(jnp.float32) + two_ref[...].astype(jnp.float32)).astype(jnp.bfloat16)


def finish_image(count, log_scale_ref, image_ref, parts_ref, loss_ref, grad_ref):
    rows, width = image_ref.shape
    total = parts_ref[:rows, :].astype(jnp.float32)
    for part in range(1, parts_ref.shape[0] // rows):
        total = total + parts_ref[part * rows : (part + 1) * rows, :].astype(jnp.float32)
    scale = jnp.exp(jnp.full((1, 1), log_scale_ref[0], jnp.float32))
    unit, norm = normed(image_ref[...])
    grad_ref[...] = project(scale * total[:, :width], unit, norm)
    loss_ref[...] = jnp.sum(total[:, width:], axis=1, keepdims=True) / count


def finish_text(log_scale_ref, text_ref, *refs):
    total = refs[0][...].astype(jnp.float32)
    for ref in refs[1:-1]:
        total = total + ref[...].astype(jnp.float32)
    scale = jnp.exp(jnp.full((1, 1), log_scale_ref[0], jnp.float32))
    unit, norm = normed(text_ref[...])
    refs[-1][...] = project(scale * total, unit, norm)


def per_device(image, text, log_scale, bias):
    rows, width = image.shape
    plane = lax.axis_size(PLANE)
    half = rows * plane
    smem = pl.BlockSpec(memory_space=pltpu.SMEM)
    vmem = pl.BlockSpec(memory_space=pltpu.VMEM)
    low = jax.ShapeDtypeStruct((rows, width), jnp.bfloat16)
    wide = jax.ShapeDtypeStruct((half, width + EXTRA), jnp.bfloat16)
    full = jax.ShapeDtypeStruct((rows, width), jnp.float32)

    image_low, text_low = call(prepare, (low, low))(image, text)
    copies = jnp.broadcast_to(image_low[None], (plane, rows, width)).reshape(half, width)
    mine = lax.all_to_all(copies, PLANE, 0, 0, tiled=True)
    texts = [text_low] + [to_behind(text_low, k) for k in range(1, SLOTS)]
    swap = [(0, 1), (1, 0)]
    (mine,) = after([mine], texts[1:])
    other = lax.ppermute(mine, "core", swap)

    place = jnp.stack([lax.axis_index("yl"), lax.axis_index(("x", "yh")) * rows]).astype(jnp.int32)
    results = call(
        score,
        (wide, wide) + (low,) * SLOTS,
        in_specs=[smem] * 3 + [vmem] * (2 + SLOTS),
        out_specs=(vmem,) * (2 + SLOTS),
        scratch_shapes=[
            pltpu.VMEM((TEXT_ROWS, width), jnp.bfloat16),
            pltpu.VMEM((2 * half, TEXT_ROWS), jnp.bfloat16),
        ],
    )(log_scale, bias, place, mine, other, *texts)
    keep, send = results[:2]
    arrived = lax.ppermute(send, "core", swap)
    summed = call(add_pair, wide)(keep, arrived)
    leaving = after(results[3:], [summed])
    back = [results[2]] + [to_owner(part, k + 1) for k, part in enumerate(leaving)]
    parts = lax.all_to_all(summed, PLANE, 0, 0, tiled=True)
    loss, grad_image = call(
        functools.partial(finish_image, float(STEPS * half)),
        (jax.ShapeDtypeStruct((rows, 1), jnp.float32), full),
        in_specs=[smem, vmem, vmem],
    )(log_scale, image, parts)
    grad_text = call(finish_text, full, in_specs=[smem] + [vmem] * (1 + SLOTS))(log_scale, text, *back)
    return (loss.reshape(rows), grad_image, grad_text)


def solution(mesh):
    axes = ("z", "yl", "x", "yh", "core")
    fine = jax.sharding.Mesh(mesh.devices.reshape(32, 2, 4, 2, 2), axes)
    rows = P(axes, None)
    return jax.shard_map(
        per_device,
        mesh=fine,
        in_specs=(rows, rows, P(), P()),
        out_specs=(P(axes), rows, rows),
        check_vma=False,
    )
```

```python
import functools

import jax
import jax.numpy as jnp
from jax import lax
from jax.experimental import pallas as pl
from jax.experimental.pallas import tpu as pltpu
from jax.sharding import PartitionSpec as P

STEPS = 8
EPS = 1e-06
PLANE = ("yl", "x", "yh")
SLOTS = 5
TEXT_ROWS = 256
EXTRA = 128
PIECES = 4
LIMIT = 8 * 1024 * 1024
WHOLE = 60 * 1024 * 1024


def call(kernel, out_shape, flops=0, limit=LIMIT, **kwargs):
    return pl.pallas_call(
        kernel,
        out_shape=out_shape,
        compiler_params=pltpu.CompilerParams(vmem_limit_bytes=limit),
        cost_estimate=pl.CostEstimate(flops=flops, bytes_accessed=flops // 512, transcendentals=0) if flops else None,
        **kwargs,
    )


def along_z(value, planes, parities=(0, 1)):
    count = lax.axis_size("z")
    pairs = [(2 * z + yl, 2 * ((z + planes) % count) + yl) for z in range(count) for yl in parities]
    return lax.ppermute(value, ("z", "yl"), pairs)


def normed(rows):
    values = rows.astype(jnp.float32)
    norm = jnp.sqrt(jnp.sum(values * values, axis=-1, keepdims=True) + EPS)
    return (values / norm, norm)


def project(unit_grad, unit, norm):
    inner = jnp.sum(unit * unit_grad, axis=-1, keepdims=True)
    return (unit_grad - unit * inner) / norm


def prepare(image_hbm, text_hbm, copies_hbm, text_low_ref, image_ref, text_ref, low_ref, in_sems, out_sems):
    fetches = [
        pltpu.make_async_copy(image_hbm, image_ref, in_sems.at[0]),
        pltpu.make_async_copy(text_hbm, text_ref, in_sems.at[1]),
    ]
    for fetch in fetches:
        fetch.start()
    fetches[0].wait()
    low_ref[...] = normed(image_ref[...])[0].astype(jnp.bfloat16)
    rows = low_ref.shape[0]
    stores = [
        pltpu.make_async_copy(low_ref, copies_hbm.at[pl.ds(part * rows, rows)], out_sems.at[part])
        for part in range(copies_hbm.shape[0] // rows)
    ]
    for store in stores:
        store.start()
    fetches[1].wait()
    text_low_ref[...] = normed(text_ref[...])[0].astype(jnp.bfloat16)
    for store in stores:
        store.wait()


def pack(*refs):
    rows, width = refs[0].shape
    for k in range(SLOTS):
        refs[-1][k * rows : (k + 1) * rows, :] = refs[k][...]
    refs[-1][SLOTS * rows :, :] = jnp.zeros((TEXT_ROWS - SLOTS * rows, width), jnp.bfloat16)


def score(
    rows, log_scale_ref, bias_ref, place_ref, image_hbm, own_hbm, other_hbm, grad_hbm, ours_hbm, theirs_hbm,
    image_ref, text_refs, coef_ref, grad_ref, ours_ref, theirs_ref, in_sems, out_sems,
):
    half, width = image_hbm.shape
    piece = half // PIECES
    spans = [pl.ds(part * piece, piece) for part in range(PIECES)]
    text_fetches = [
        pltpu.make_async_copy(text_hbm, text_refs.at[side], in_sems.at[side])
        for side, text_hbm in enumerate((own_hbm, other_hbm))
    ]
    image_fetches = [
        pltpu.make_async_copy(image_hbm.at[span], image_ref.at[span], in_sems.at[2 + part])
        for part, span in enumerate(spans)
    ]
    for fetch in text_fetches + image_fetches:
        fetch.start()
    scale = jnp.exp(jnp.full((1, 1), log_scale_ref[0], jnp.float32))
    parity, place = place_ref[0], place_ref[1]
    cols = lax.broadcasted_iota(jnp.int32, (1, TEXT_ROWS), 1)
    slot = jnp.zeros((1, TEXT_ROWS), jnp.int32)
    for k in range(1, SLOTS):
        slot = slot + (cols >= k * rows).astype(jnp.int32)
    lane = lax.broadcasted_iota(jnp.int32, (piece, EXTRA), 1)
    row_ids = lax.broadcasted_iota(jnp.int32, (piece, TEXT_ROWS), 0)
    col_ids = lax.broadcasted_iota(jnp.int32, (piece, TEXT_ROWS), 1)
    for fetch in text_fetches:
        fetch.wait()
    stores = []
    for part, span in enumerate(spans):
        image_fetches[part].wait()
        start = part * piece
        image = image_ref[start : start + piece, :]
        block = start // (half // 2)
        offset = 2 * slot + parity - block
        scored = ((offset >= 0) & (offset < STEPS) & (cols < SLOTS * rows)).astype(jnp.float32)
        loss = jnp.zeros((piece, 1), jnp.float32)
        grad = jnp.zeros((piece, width), jnp.float32)
        for side in range(2):
            text = text_refs[side]
            logit = scale * lax.dot_general(
                image, text, (((1,), (1,)), ((), ())), preferred_element_type=jnp.float32
            ) + bias_ref[0]
            coef = 0.5 * jnp.tanh(0.5 * logit) + 0.5
            term = -jnp.log(1.0 - coef)
            if side == 0:
                positive = (row_ids + start == col_ids + parity * (half // 2) + place) & (col_ids < rows)
                term = term - jnp.where(positive, logit, 0.0)
                coef = coef - jnp.where(positive, 1.0, 0.0)
            loss = loss + jnp.sum(term * scored, axis=1, keepdims=True)
            coef = (coef * scored).astype(jnp.bfloat16)
            coef_ref[side, start : start + piece, :] = coef
            grad = grad + jnp.dot(coef, text, preferred_element_type=jnp.float32)
        loss_high = loss.astype(jnp.bfloat16).astype(jnp.float32)
        extra = jnp.where(lane == 0, loss_high, jnp.where(lane == 1, loss - loss_high, 0.0))
        grad_ref[start : start + piece, :width] = grad.astype(jnp.bfloat16)
        grad_ref[start : start + piece, width:] = extra.astype(jnp.bfloat16)
        stores.append(pltpu.make_async_copy(grad_ref.at[span], grad_hbm.at[span], out_sems.at[part]))
        stores[-1].start()
    for side, (text_ref, text_hbm) in enumerate(((ours_ref, ours_hbm), (theirs_ref, theirs_hbm))):
        terms = lax.dot_general(
            coef_ref[side], image_ref[...], (((0,), (0,)), ((), ())), preferred_element_type=jnp.float32
        )
        text_ref[...] = terms[: SLOTS * rows].astype(text_ref.dtype)
        stores.append(pltpu.make_async_copy(text_ref, text_hbm, out_sems.at[PIECES + side]))
        stores[-1].start()
    for store in stores:
        store.wait()


def join(ours_ref, theirs_ref, *grad_refs):
    rows = grad_refs[0].shape[0]
    for k, grad_ref in enumerate(grad_refs):
        here = slice(k * rows, (k + 1) * rows)
        grad_ref[...] = (ours_ref[here, :] + theirs_ref[here, :].astype(jnp.float32)).astype(jnp.bfloat16)


def add(*refs):
    total = refs[0][...].astype(jnp.float32)
    for ref in refs[1:-1]:
        total = total + ref[...].astype(jnp.float32)
    refs[-1][...] = total.astype(jnp.bfloat16)


def finish_image(count, log_scale_ref, image_hbm, parts_ref, loss_ref, grad_ref, image_ref, sem):
    fetch = pltpu.make_async_copy(image_hbm, image_ref, sem)
    fetch.start()
    rows, width = image_ref.shape
    total = parts_ref[:rows, :].astype(jnp.float32)
    for part in range(1, parts_ref.shape[0] // rows):
        total = total + parts_ref[part * rows : (part + 1) * rows, :].astype(jnp.float32)
    scale = jnp.exp(jnp.full((1, 1), log_scale_ref[0], jnp.float32))
    loss = lax.dot_general(
        jnp.full((8, EXTRA), 1.0 / count, jnp.float32),
        total[:, width:],
        (((1,), (1,)), ((), ())),
        precision=lax.Precision.HIGHEST,
        preferred_element_type=jnp.float32,
    )
    loss_ref[...] = loss[0]
    fetch.wait()
    unit, norm = normed(image_ref[...])
    grad_ref[...] = project(scale * total[:, :width], unit, norm)


def finish_text(log_scale_ref, text_ref, *refs):
    total = refs[0][...].astype(jnp.float32)
    for ref in refs[1:-1]:
        total = total + ref[...].astype(jnp.float32)
    scale = jnp.exp(jnp.full((1, 1), log_scale_ref[0], jnp.float32))
    unit, norm = normed(text_ref[...])
    refs[-1][...] = project(scale * total, unit, norm)


def per_device(image, text, log_scale, bias):
    rows, width = image.shape
    plane = lax.axis_size(PLANE)
    half = rows * plane
    smem = pl.BlockSpec(memory_space=pltpu.SMEM)
    vmem = pl.BlockSpec(memory_space=pltpu.VMEM)
    hbm = pl.BlockSpec(memory_space=pltpu.HBM)
    low = jax.ShapeDtypeStruct((rows, width), jnp.bfloat16)
    wide = jax.ShapeDtypeStruct((half, width + EXTRA), jnp.bfloat16)
    full = jax.ShapeDtypeStruct((rows, width), jnp.float32)
    swap = [(0, 1), (1, 0)]
    dma = pltpu.SemaphoreType.DMA

    copies, text_low = call(
        prepare,
        (jax.ShapeDtypeStruct((half, width), jnp.bfloat16), low),
        in_specs=[hbm, hbm],
        out_specs=(hbm, vmem),
        scratch_shapes=[pltpu.VMEM((rows, width), jnp.bfloat16)] * 3 + [dma((2,)), dma((plane,))],
        limit=WHOLE,
    )(image, text)
    mine = lax.all_to_all(copies, PLANE, 0, 0, tiled=True)
    one = along_z(text_low, -1)
    two = along_z(text_low, -2)
    three = along_z(two, -1)
    four = along_z(two, -2, (0,))
    own = call(pack, jax.ShapeDtypeStruct((TEXT_ROWS, width), jnp.bfloat16))(text_low, one, two, three, four)
    other = lax.ppermute(own, "core", swap)

    place = jnp.stack([lax.axis_index("yl"), lax.axis_index(("x", "yh")) * rows]).astype(jnp.int32)
    packed = (SLOTS * rows, width)
    grads, ours, theirs = call(
        functools.partial(score, rows),
        (wide, jax.ShapeDtypeStruct(packed, jnp.float32), jax.ShapeDtypeStruct(packed, jnp.bfloat16)),
        12 * half * TEXT_ROWS * width,
        in_specs=[smem] * 3 + [hbm] * 3,
        out_specs=(hbm,) * 3,
        scratch_shapes=[
            pltpu.VMEM((half, width), jnp.bfloat16),
            pltpu.VMEM((2, TEXT_ROWS, width), jnp.bfloat16),
            pltpu.VMEM((2, half, TEXT_ROWS), jnp.bfloat16),
            pltpu.VMEM((half, width + EXTRA), jnp.bfloat16),
            pltpu.VMEM(packed, jnp.float32),
            pltpu.VMEM(packed, jnp.bfloat16),
            dma((2 + PIECES,)),
            dma((2 + PIECES,)),
        ],
        limit=WHOLE,
    )(log_scale, bias, place, mine, own, other)
    parts = lax.all_to_all(grads, PLANE, 0, 0, tiled=True)
    terms = call(join, (low,) * SLOTS)(ours, lax.ppermute(theirs, "core", swap))
    middle = call(add, low)(terms[2], along_z(terms[3], 1), along_z(terms[4], 2, (0,)))
    back = [terms[0], along_z(terms[1], 1), along_z(middle, 2)]
    loss, grad_image = call(
        functools.partial(finish_image, float(STEPS * half)),
        (jax.ShapeDtypeStruct((rows,), jnp.float32), full),
        in_specs=[smem, hbm, vmem],
        scratch_shapes=[pltpu.VMEM((rows, width), jnp.bfloat16), dma],
    )(log_scale, image, parts)
    grad_text = call(finish_text, full, in_specs=[smem] + [vmem] * (1 + len(back)))(log_scale, text, *back)
    return (loss, grad_image, grad_text)


def solution(mesh):
    axes = ("z", "yl", "x", "yh", "core")
    fine = jax.sharding.Mesh(mesh.devices.reshape(32, 2, 4, 2, 2), axes)
    rows = P(axes, None)
    return jax.shard_map(
        per_device,
        mesh=fine,
        in_specs=(rows, rows, P(), P()),
        out_specs=(P(axes), rows, rows),
        check_vma=False,
    )
```

```python
import functools

import jax
import jax.numpy as jnp
from jax import lax
from jax.experimental import pallas as pl
from jax.experimental.pallas import tpu as pltpu
from jax.sharding import PartitionSpec as P

STEPS = 8
EPS = 1e-06
PLANE = ("yl", "x", "yh")
SLOTS = 5
PACKED = 256
EXTRA = 128
PIECES = 4
LIMIT = 8 * 1024 * 1024
WHOLE = 60 * 1024 * 1024


def call(kernel, out_shape, flops=0, limit=LIMIT, **kwargs):
    return pl.pallas_call(
        kernel,
        out_shape=out_shape,
        compiler_params=pltpu.CompilerParams(vmem_limit_bytes=limit),
        cost_estimate=pl.CostEstimate(flops=flops, bytes_accessed=flops // 512, transcendentals=0) if flops else None,
        **kwargs,
    )


def along_z(value, planes, parities=(0, 1)):
    count = lax.axis_size("z")
    pairs = [(2 * z + yl, 2 * ((z + planes) % count) + yl) for z in range(count) for yl in parities]
    return lax.ppermute(value, ("z", "yl"), pairs)


def normed(rows):
    values = rows.astype(jnp.float32)
    norm = jnp.sqrt(jnp.sum(values * values, axis=-1, keepdims=True) + EPS)
    return (values / norm, norm)


def project(unit_grad, unit, norm):
    inner = jnp.sum(unit * unit_grad, axis=-1, keepdims=True)
    return (unit_grad - unit * inner) / norm


def prepare(still_hbm, moving_hbm, copies_hbm, low_hbm, still_ref, moving_ref, copy_ref, low_ref, in_sems, out_sems):
    fetches = [
        pltpu.make_async_copy(still_hbm, still_ref, in_sems.at[0]),
        pltpu.make_async_copy(moving_hbm, moving_ref, in_sems.at[1]),
    ]
    for fetch in fetches:
        fetch.start()
    fetches[0].wait()
    copy_ref[...] = normed(still_ref[...])[0].astype(jnp.bfloat16)
    rows = copy_ref.shape[0]
    stores = [
        pltpu.make_async_copy(copy_ref, copies_hbm.at[pl.ds(part * rows, rows)], out_sems.at[part])
        for part in range(copies_hbm.shape[0] // rows)
    ]
    for store in stores:
        store.start()
    fetches[1].wait()
    low_ref[...] = normed(moving_ref[...])[0].astype(jnp.bfloat16)
    stores.append(pltpu.make_async_copy(low_ref, low_hbm, in_sems.at[2]))
    stores[-1].start()
    for store in stores:
        store.wait()


def pack(*refs):
    rows, width = refs[0].shape
    for k in range(SLOTS):
        refs[-1][k * rows : (k + 1) * rows, :] = refs[k][...]
    refs[-1][SLOTS * rows :, :] = jnp.zeros((PACKED - SLOTS * rows, width), jnp.bfloat16)


def loss_lanes(loss):
    high = loss.astype(jnp.bfloat16).astype(jnp.float32)
    lane = lax.broadcasted_iota(jnp.int32, (loss.shape[0], EXTRA), 1)
    return jnp.where(lane == 0, high, jnp.where(lane == 1, loss - high, 0.0))


def score(
    rows, log_scale_ref, bias_ref, place_ref, text_hbm, own_hbm, other_hbm, grad_hbm, ours_hbm, theirs_hbm,
    text_ref, image_refs, coef_ref, grad_ref, ours_ref, theirs_ref, in_sems, out_sems,
):
    half, width = text_hbm.shape
    piece = half // PIECES
    spans = [pl.ds(part * piece, piece) for part in range(PIECES)]
    image_fetches = [
        pltpu.make_async_copy(image_hbm, image_refs.at[side], in_sems.at[side])
        for side, image_hbm in enumerate((own_hbm, other_hbm))
    ]
    text_fetches = [
        pltpu.make_async_copy(text_hbm.at[span], text_ref.at[span], in_sems.at[2 + part])
        for part, span in enumerate(spans)
    ]
    for fetch in image_fetches + text_fetches:
        fetch.start()
    scale = jnp.exp(jnp.full((1, 1), log_scale_ref[0], jnp.float32))
    parity, place = place_ref[0], place_ref[1]
    cols = lax.broadcasted_iota(jnp.int32, (1, PACKED), 1)
    slot = jnp.zeros((1, PACKED), jnp.int32)
    for k in range(1, SLOTS):
        slot = slot + (cols >= k * rows).astype(jnp.int32)
    row_ids = lax.broadcasted_iota(jnp.int32, (piece, PACKED), 0)
    col_ids = lax.broadcasted_iota(jnp.int32, (piece, PACKED), 1)
    for fetch in image_fetches:
        fetch.wait()

    def products(part):
        text_fetches[part].wait()
        text = text_ref[part * piece : (part + 1) * piece, :]
        return [
            lax.dot_general(text, image_refs[side], (((1,), (1,)), ((), ())), preferred_element_type=jnp.float32)
            for side in range(2)
        ]

    stores = []
    losses = [jnp.zeros((1, PACKED), jnp.float32)] * 2
    ahead = products(0)
    for part, span in enumerate(spans):
        start = part * piece
        block = start // (half // 2)
        offset = 2 * slot + block - parity
        scored = ((offset >= 0) & (offset < STEPS) & (cols < SLOTS * rows)).astype(jnp.float32)
        now = ahead
        if part + 1 < PIECES:
            ahead = products(part + 1)
        grad = jnp.zeros((piece, width), jnp.float32)
        for side in range(2):
            logit = scale * now[side] + bias_ref[0]
            coef = 0.5 * jnp.tanh(0.5 * logit) + 0.5
            term = -jnp.log(1.0 - coef)
            if side == 0:
                positive = (row_ids + start == col_ids + parity * (half // 2) + place) & (col_ids < rows)
                term = term - jnp.where(positive, logit, 0.0)
                coef = coef - jnp.where(positive, 1.0, 0.0)
            losses[side] = losses[side] + scored * jnp.sum(term, axis=0, keepdims=True)
            coef = (coef * scored).astype(jnp.bfloat16)
            coef_ref[side, start : start + piece, :] = coef
            grad = grad + jnp.dot(coef, image_refs[side], preferred_element_type=jnp.float32)
        grad_ref[start : start + piece, :] = grad.astype(jnp.bfloat16)
        stores.append(pltpu.make_async_copy(grad_ref.at[span], grad_hbm.at[span], out_sems.at[part]))
        stores[-1].start()
    for side, (image_ref, image_hbm) in enumerate(((ours_ref, ours_hbm), (theirs_ref, theirs_hbm))):
        terms = lax.dot_general(
            coef_ref[side], text_ref[...], (((0,), (0,)), ((), ())), preferred_element_type=jnp.float32
        )
        loss = jnp.transpose(jnp.broadcast_to(losses[side], (EXTRA, PACKED)))[: SLOTS * rows, :1]
        image_ref[:, :width] = terms[: SLOTS * rows].astype(image_ref.dtype)
        image_ref[:, width:] = loss_lanes(loss).astype(image_ref.dtype)
        stores.append(pltpu.make_async_copy(image_ref, image_hbm, out_sems.at[PIECES + side]))
        stores[-1].start()
    for store in stores:
        store.wait()


def store_sum(out_ref, total):
    width = total.shape[1] - EXTRA
    out_ref[:, :width] = total[:, :width].astype(jnp.bfloat16)
    out_ref[:, width:] = loss_lanes(jnp.sum(total[:, width:], axis=1, keepdims=True)).astype(jnp.bfloat16)


def join(ours_ref, theirs_ref, *grad_refs):
    rows = grad_refs[0].shape[0]
    for k, grad_ref in enumerate(grad_refs):
        here = slice(k * rows, (k + 1) * rows)
        store_sum(grad_ref, ours_ref[here, :] + theirs_ref[here, :].astype(jnp.float32))


def sum_of(refs):
    total = refs[0][...].astype(jnp.float32)
    for ref in refs[1:]:
        total = total + ref[...].astype(jnp.float32)
    return total


def add(*refs):
    store_sum(refs[-1], sum_of(refs[:-1]))


def finish_image(count, log_scale_ref, image_ref, *refs):
    grads, (loss_ref, out_ref) = refs[:-2], refs[-2:]
    width = image_ref.shape[1]
    total = sum_of(grads)
    loss = lax.dot_general(
        jnp.full((8, EXTRA), 1.0 / count, jnp.float32),
        total[:, width:],
        (((1,), (1,)), ((), ())),
        precision=lax.Precision.HIGHEST,
        preferred_element_type=jnp.float32,
    )
    loss_ref[...] = loss[0]
    scale = jnp.exp(jnp.full((1, 1), log_scale_ref[0], jnp.float32))
    unit, norm = normed(image_ref[...])
    out_ref[...] = project(scale * total[:, :width], unit, norm)


def finish_text(log_scale_ref, text_hbm, parts_ref, grad_ref, text_ref, sem):
    fetch = pltpu.make_async_copy(text_hbm, text_ref, sem)
    fetch.start()
    rows = text_ref.shape[0]
    total = parts_ref[:rows, :].astype(jnp.float32)
    for part in range(1, parts_ref.shape[0] // rows):
        total = total + parts_ref[part * rows : (part + 1) * rows, :].astype(jnp.float32)
    scale = jnp.exp(jnp.full((1, 1), log_scale_ref[0], jnp.float32))
    fetch.wait()
    unit, norm = normed(text_ref[...])
    grad_ref[...] = project(scale * total, unit, norm)


def per_device(image, text, log_scale, bias):
    rows, width = image.shape
    plane = lax.axis_size(PLANE)
    half = rows * plane
    smem = pl.BlockSpec(memory_space=pltpu.SMEM)
    vmem = pl.BlockSpec(memory_space=pltpu.VMEM)
    hbm = pl.BlockSpec(memory_space=pltpu.HBM)
    low = jax.ShapeDtypeStruct((rows, width), jnp.bfloat16)
    wide = jax.ShapeDtypeStruct((rows, width + EXTRA), jnp.bfloat16)
    gathered = jax.ShapeDtypeStruct((half, width), jnp.bfloat16)
    full = jax.ShapeDtypeStruct((rows, width), jnp.float32)
    swap = [(0, 1), (1, 0)]
    dma = pltpu.SemaphoreType.DMA

    copies, image_low = call(
        prepare,
        (gathered, low),
        in_specs=[hbm, hbm],
        out_specs=(hbm, hbm),
        scratch_shapes=[pltpu.VMEM((rows, width), jnp.bfloat16)] * 4 + [dma((3,)), dma((plane,))],
        limit=WHOLE,
    )(text, image)
    texts = lax.all_to_all(copies, PLANE, 0, 0, tiled=True)
    one = along_z(image_low, 1)
    two = along_z(image_low, 2)
    three = along_z(two, 1)
    four = along_z(two, 2, (1,))
    own = call(pack, jax.ShapeDtypeStruct((PACKED, width), jnp.bfloat16))(image_low, one, two, three, four)
    other = lax.ppermute(own, "core", swap)

    place = jnp.stack([lax.axis_index("yl"), lax.axis_index(("x", "yh")) * rows]).astype(jnp.int32)
    packed = (SLOTS * rows, width + EXTRA)
    grads, ours, theirs = call(
        functools.partial(score, rows),
        (gathered, jax.ShapeDtypeStruct(packed, jnp.float32), jax.ShapeDtypeStruct(packed, jnp.bfloat16)),
        12 * half * PACKED * width,
        in_specs=[smem] * 3 + [hbm] * 3,
        out_specs=(hbm,) * 3,
        scratch_shapes=[
            pltpu.VMEM((half, width), jnp.bfloat16),
            pltpu.VMEM((2, PACKED, width), jnp.bfloat16),
            pltpu.VMEM((2, half, PACKED), jnp.bfloat16),
            pltpu.VMEM((half, width), jnp.bfloat16),
            pltpu.VMEM(packed, jnp.float32),
            pltpu.VMEM(packed, jnp.bfloat16),
            dma((2 + PIECES,)),
            dma((2 + PIECES,)),
        ],
        limit=WHOLE,
    )(log_scale, bias, place, texts, own, other)
    parts = lax.all_to_all(grads, PLANE, 0, 0, tiled=True)
    terms = call(join, (wide,) * SLOTS)(ours, lax.ppermute(theirs, "core", swap))
    middle = call(add, wide)(terms[2], along_z(terms[3], -1), along_z(terms[4], -2, (1,)))
    back = [terms[0], along_z(terms[1], -1), along_z(middle, -2)]
    loss, grad_image = call(
        functools.partial(finish_image, float(STEPS * half)),
        (jax.ShapeDtypeStruct((rows,), jnp.float32), full),
        in_specs=[smem] + [vmem] * (1 + len(back)),
    )(log_scale, image, *back)
    grad_text = call(
        finish_text,
        full,
        in_specs=[smem, hbm, vmem],
        scratch_shapes=[pltpu.VMEM((rows, width), jnp.bfloat16), dma],
    )(log_scale, text, parts)
    return (loss, grad_image, grad_text)


def solution(mesh):
    axes = ("z", "yl", "x", "yh", "core")
    fine = jax.sharding.Mesh(mesh.devices.reshape(32, 2, 4, 2, 2), axes)
    rows = P(axes, None)
    return jax.shard_map(
        per_device,
        mesh=fine,
        in_specs=(rows, rows, P(), P()),
        out_specs=(P(axes), rows, rows),
        check_vma=False,
    )
```

```python
import functools

import jax
import jax.numpy as jnp
from jax import lax
from jax.experimental import pallas as pl
from jax.experimental.pallas import tpu as pltpu
from jax.sharding import PartitionSpec as P

STEPS = 8
EPS = 1e-06
PLANE = ("yl", "x", "yh")
SLOTS = 5
PACKED = 256
EXTRA = 128
PIECES = 2
RUNS = 4
LIMIT = 8 * 1024 * 1024
WHOLE = 60 * 1024 * 1024


def call(kernel, out_shape, flops=0, limit=LIMIT, **kwargs):
    return pl.pallas_call(
        kernel,
        out_shape=out_shape,
        compiler_params=pltpu.CompilerParams(vmem_limit_bytes=limit),
        cost_estimate=pl.CostEstimate(flops=flops, bytes_accessed=flops // 512, transcendentals=0) if flops else None,
        **kwargs,
    )


def along_z(value, planes, parities=(0, 1)):
    count = lax.axis_size("z")
    pairs = [(2 * z + yl, 2 * ((z + planes) % count) + yl) for z in range(count) for yl in parities]
    return lax.ppermute(value, ("z", "yl"), pairs)


def normed(rows):
    values = rows.astype(jnp.float32)
    norm = jnp.sqrt(jnp.sum(values * values, axis=-1, keepdims=True) + EPS)
    return (values / norm, norm)


def project(unit_grad, unit, norm):
    inner = jnp.sum(unit * unit_grad, axis=-1, keepdims=True)
    return (unit_grad - unit * inner) / norm


def prepare(still_hbm, moving_hbm, copies_hbm, low_hbm, still_ref, moving_ref, copy_ref, low_ref, in_sems, out_sems):
    fetches = [
        pltpu.make_async_copy(still_hbm, still_ref, in_sems.at[0]),
        pltpu.make_async_copy(moving_hbm, moving_ref, in_sems.at[1]),
    ]
    for fetch in fetches:
        fetch.start()
    fetches[0].wait()
    copy_ref[...] = normed(still_ref[...])[0].astype(jnp.bfloat16)
    rows = copy_ref.shape[0]
    stores = [
        pltpu.make_async_copy(copy_ref, copies_hbm.at[pl.ds(part * rows, rows)], out_sems.at[part])
        for part in range(copies_hbm.shape[0] // rows)
    ]
    for store in stores:
        store.start()
    fetches[1].wait()
    low_ref[...] = normed(moving_ref[...])[0].astype(jnp.bfloat16)
    stores.append(pltpu.make_async_copy(low_ref, low_hbm, in_sems.at[2]))
    stores[-1].start()
    for store in stores:
        store.wait()


def pack(*refs):
    rows, width = refs[0].shape
    for k in range(SLOTS):
        refs[-1][k * rows : (k + 1) * rows, :] = refs[k][...]
    refs[-1][SLOTS * rows :, :] = jnp.zeros((PACKED - SLOTS * rows, width), jnp.bfloat16)


def chunks(count, source, target, sems, first=0):
    rows = source.shape[0] // count
    return [
        pltpu.make_async_copy(
            source.at[pl.ds(part * rows, rows)], target.at[pl.ds(part * rows, rows)], sems.at[first + part]
        )
        for part in range(count)
    ]


def loss_lanes(loss):
    high = loss.astype(jnp.bfloat16).astype(jnp.float32)
    lane = lax.broadcasted_iota(jnp.int32, (loss.shape[0], EXTRA), 1)
    return jnp.where(lane == 0, high, jnp.where(lane == 1, loss - high, 0.0))


def score(
    rows, log_scale_ref, bias_ref, place_ref, text_hbm, own_hbm, other_hbm, grad_hbm, ours_hbm, theirs_hbm,
    text_ref, image_ref, coef_ref, grad_ref, ours_ref, theirs_ref, in_sems, out_sems,
):
    half, width = text_hbm.shape
    piece = half // PIECES
    image_fetches = chunks(RUNS, own_hbm, image_ref.at[pl.ds(0, PACKED)], in_sems) + chunks(
        RUNS, other_hbm, image_ref.at[pl.ds(PACKED, PACKED)], in_sems, RUNS
    )
    text_fetches = chunks(2 * RUNS, text_hbm, text_ref, in_sems, 2 * RUNS)
    for fetch in image_fetches + text_fetches:
        fetch.start()
    scale = jnp.exp(jnp.full((1, 1), log_scale_ref[0], jnp.float32))
    parity, place = place_ref[0], place_ref[1]
    cols = lax.broadcasted_iota(jnp.int32, (1, PACKED), 1)
    slot = jnp.zeros((1, PACKED), jnp.int32)
    for k in range(1, SLOTS):
        slot = slot + (cols >= k * rows).astype(jnp.int32)
    row_ids = lax.broadcasted_iota(jnp.int32, (piece, PACKED), 0)
    col_ids = lax.broadcasted_iota(jnp.int32, (piece, PACKED), 1)
    for fetch in image_fetches:
        fetch.wait()

    def product(part):
        for fetch in text_fetches[part * 2 * RUNS // PIECES : (part + 1) * 2 * RUNS // PIECES]:
            fetch.wait()
        return lax.dot_general(
            text_ref[part * piece : (part + 1) * piece, :],
            image_ref[...],
            (((1,), (1,)), ((), ())),
            preferred_element_type=jnp.float32,
        )

    losses = [jnp.zeros((1, PACKED), jnp.float32)] * 2
    ahead = product(0)
    for part in range(PIECES):
        start = part * piece
        block = start // (half // 2)
        offset = 2 * slot + block - parity
        scored = ((offset >= 0) & (offset < STEPS) & (cols < SLOTS * rows)).astype(jnp.float32)
        now = ahead
        if part + 1 < PIECES:
            ahead = product(part + 1)
        for side in range(2):
            here = slice(side * PACKED, (side + 1) * PACKED)
            logit = scale * now[:, here] + bias_ref[0]
            coef = 0.5 * jnp.tanh(0.5 * logit) + 0.5
            term = -jnp.log(1.0 - coef)
            if side == 0:
                positive = (row_ids + start == col_ids + parity * (half // 2) + place) & (col_ids < rows)
                term = term - jnp.where(positive, logit, 0.0)
                coef = coef - jnp.where(positive, 1.0, 0.0)
            losses[side] = losses[side] + scored * jnp.sum(term, axis=0, keepdims=True)
            coef_ref[start : start + piece, here] = (coef * scored).astype(jnp.bfloat16)
    stores = []
    for side, (out_ref, out_hbm) in enumerate(((ours_ref, ours_hbm), (theirs_ref, theirs_hbm))):
        terms = lax.dot_general(
            coef_ref[:, side * PACKED : (side + 1) * PACKED],
            text_ref[...],
            (((0,), (0,)), ((), ())),
            preferred_element_type=jnp.float32,
        )
        loss = jnp.transpose(jnp.broadcast_to(losses[side], (EXTRA, PACKED)))[: SLOTS * rows, :1]
        out_ref[:, :width] = terms[: SLOTS * rows].astype(jnp.bfloat16)
        out_ref[:, width:] = loss_lanes(loss).astype(jnp.bfloat16)
        stores += chunks(SLOTS, out_ref, out_hbm, out_sems, side * SLOTS)
        for store in stores[-SLOTS:]:
            store.start()
    run = half // RUNS
    for part in range(RUNS):
        here = slice(part * run, (part + 1) * run)
        grad_ref[here, :] = jnp.dot(coef_ref[here, :], image_ref[...], preferred_element_type=jnp.float32).astype(
            jnp.bfloat16
        )
        span = pl.ds(part * run, run)
        stores.append(pltpu.make_async_copy(grad_ref.at[span], grad_hbm.at[span], out_sems.at[2 * SLOTS + part]))
        stores[-1].start()
    for store in stores:
        store.wait()


def store_sum(out_ref, total):
    width = total.shape[1] - EXTRA
    out_ref[:, :width] = total[:, :width].astype(jnp.bfloat16)
    out_ref[:, width:] = loss_lanes(jnp.sum(total[:, width:], axis=1, keepdims=True)).astype(jnp.bfloat16)


def join(ours_ref, theirs_ref, *grad_refs):
    rows = grad_refs[0].shape[0]
    for k, grad_ref in enumerate(grad_refs):
        here = slice(k * rows, (k + 1) * rows)
        store_sum(grad_ref, sum_of([ours_ref.at[here], theirs_ref.at[here]]))


def sum_of(refs):
    total = refs[0][...].astype(jnp.float32)
    for ref in refs[1:]:
        total = total + ref[...].astype(jnp.float32)
    return total


def add(*refs):
    store_sum(refs[-1], sum_of(refs[:-1]))


def finish_image(count, log_scale_ref, image_ref, *refs):
    grads, (loss_ref, out_ref) = refs[:-2], refs[-2:]
    width = image_ref.shape[1]
    total = sum_of(grads)
    loss = lax.dot_general(
        jnp.full((8, EXTRA), 1.0 / count, jnp.float32),
        total[:, width:],
        (((1,), (1,)), ((), ())),
        precision=lax.Precision.HIGHEST,
        preferred_element_type=jnp.float32,
    )
    loss_ref[...] = loss[0]
    scale = jnp.exp(jnp.full((1, 1), log_scale_ref[0], jnp.float32))
    unit, norm = normed(image_ref[...])
    out_ref[...] = project(scale * total[:, :width], unit, norm)


def finish_text(log_scale_ref, text_hbm, parts_ref, grad_ref, text_ref, sem):
    fetch = pltpu.make_async_copy(text_hbm, text_ref, sem)
    fetch.start()
    rows = text_ref.shape[0]
    total = parts_ref[:rows, :].astype(jnp.float32)
    for part in range(1, parts_ref.shape[0] // rows):
        total = total + parts_ref[part * rows : (part + 1) * rows, :].astype(jnp.float32)
    scale = jnp.exp(jnp.full((1, 1), log_scale_ref[0], jnp.float32))
    fetch.wait()
    unit, norm = normed(text_ref[...])
    grad_ref[...] = project(scale * total, unit, norm)


def per_device(image, text, log_scale, bias):
    rows, width = image.shape
    plane = lax.axis_size(PLANE)
    half = rows * plane
    smem = pl.BlockSpec(memory_space=pltpu.SMEM)
    vmem = pl.BlockSpec(memory_space=pltpu.VMEM)
    hbm = pl.BlockSpec(memory_space=pltpu.HBM)
    low = jax.ShapeDtypeStruct((rows, width), jnp.bfloat16)
    wide = jax.ShapeDtypeStruct((rows, width + EXTRA), jnp.bfloat16)
    gathered = jax.ShapeDtypeStruct((half, width), jnp.bfloat16)
    full = jax.ShapeDtypeStruct((rows, width), jnp.float32)
    swap = [(0, 1), (1, 0)]
    dma = pltpu.SemaphoreType.DMA

    copies, image_low = call(
        prepare,
        (gathered, low),
        in_specs=[hbm, hbm],
        out_specs=(hbm, hbm),
        scratch_shapes=[pltpu.VMEM((rows, width), jnp.bfloat16)] * 4 + [dma((3,)), dma((plane,))],
        limit=WHOLE,
    )(text, image)
    texts = lax.all_to_all(copies, PLANE, 0, 0, tiled=True)
    one = along_z(image_low, 1)
    two = along_z(image_low, 2)
    three = along_z(two, 1)
    four = along_z(two, 2, (1,))
    own = call(pack, jax.ShapeDtypeStruct((PACKED, width), jnp.bfloat16))(image_low, one, two, three, four)
    other = lax.ppermute(own, "core", swap)

    place = jnp.stack([lax.axis_index("yl"), lax.axis_index(("x", "yh")) * rows]).astype(jnp.int32)
    packed = (SLOTS * rows, width + EXTRA)
    grads, ours, theirs = call(
        functools.partial(score, rows),
        (gathered, jax.ShapeDtypeStruct(packed, jnp.bfloat16), jax.ShapeDtypeStruct(packed, jnp.bfloat16)),
        12 * half * PACKED * width,
        in_specs=[smem] * 3 + [hbm] * 3,
        out_specs=(hbm,) * 3,
        scratch_shapes=[
            pltpu.VMEM((half, width), jnp.bfloat16),
            pltpu.VMEM((2 * PACKED, width), jnp.bfloat16),
            pltpu.VMEM((half, 2 * PACKED), jnp.bfloat16),
            pltpu.VMEM((half, width), jnp.bfloat16),
            pltpu.VMEM(packed, jnp.bfloat16),
            pltpu.VMEM(packed, jnp.bfloat16),
            dma((4 * RUNS,)),
            dma((2 * SLOTS + RUNS,)),
        ],
        limit=WHOLE,
    )(log_scale, bias, place, texts, own, other)
    parts = lax.all_to_all(grads, PLANE, 0, 0, tiled=True)
    terms = call(join, (wide,) * SLOTS)(ours, lax.ppermute(theirs, "core", swap))
    middle = call(add, wide)(terms[2], along_z(terms[3], -1), along_z(terms[4], -2, (1,)))
    back = [terms[0], along_z(terms[1], -1), along_z(middle, -2)]
    loss, grad_image = call(
        functools.partial(finish_image, float(STEPS * half)),
        (jax.ShapeDtypeStruct((rows,), jnp.float32), full),
        in_specs=[smem] + [vmem] * (1 + len(back)),
    )(log_scale, image, *back)
    grad_text = call(
        finish_text,
        full,
        in_specs=[smem, hbm, vmem],
        scratch_shapes=[pltpu.VMEM((rows, width), jnp.bfloat16), dma],
    )(log_scale, text, parts)
    return (loss, grad_image, grad_text)


def solution(mesh):
    axes = ("z", "yl", "x", "yh", "core")
    fine = jax.sharding.Mesh(mesh.devices.reshape(32, 2, 4, 2, 2), axes)
    rows = P(axes, None)
    return jax.shard_map(
        per_device,
        mesh=fine,
        in_specs=(rows, rows, P(), P()),
        out_specs=(P(axes), rows, rows),
        check_vma=False,
    )
```

```python
import functools

import jax
import jax.numpy as jnp
from jax import lax
from jax.experimental import pallas as pl
from jax.experimental.pallas import tpu as pltpu
from jax.sharding import PartitionSpec as P

STEPS = 8
EPS = 1e-06
PLANE = ("yl", "x", "yh")
SLOTS = 5
PACKED = 256
EXTRA = 128
PIECES = 2
LIMIT = 8 * 1024 * 1024
WHOLE = 60 * 1024 * 1024


def call(kernel, out_shape, flops=0, limit=LIMIT, **kwargs):
    return pl.pallas_call(
        kernel,
        out_shape=out_shape,
        compiler_params=pltpu.CompilerParams(vmem_limit_bytes=limit),
        cost_estimate=pl.CostEstimate(flops=flops, bytes_accessed=flops // 512, transcendentals=0) if flops else None,
        **kwargs,
    )


def along_z(value, planes, parities=(0, 1)):
    count = lax.axis_size("z")
    pairs = [(2 * z + yl, 2 * ((z + planes) % count) + yl) for z in range(count) for yl in parities]
    return lax.ppermute(value, ("z", "yl"), pairs)


def normed(rows):
    values = rows.astype(jnp.float32)
    norm = jnp.sqrt(jnp.sum(values * values, axis=-1, keepdims=True) + EPS)
    return (values / norm, norm)


def project(unit_grad, unit, norm):
    inner = jnp.sum(unit * unit_grad, axis=-1, keepdims=True)
    return (unit_grad - unit * inner) / norm


def prepare(still_hbm, moving_hbm, copies_hbm, low_hbm, still_ref, moving_ref, copy_ref, low_ref, in_sems, out_sems):
    fetches = [
        pltpu.make_async_copy(still_hbm, still_ref, in_sems.at[0]),
        pltpu.make_async_copy(moving_hbm, moving_ref, in_sems.at[1]),
    ]
    for fetch in fetches:
        fetch.start()
    fetches[0].wait()
    copy_ref[...] = normed(still_ref[...])[0].astype(jnp.bfloat16)
    rows = copy_ref.shape[0]
    stores = [
        pltpu.make_async_copy(copy_ref, copies_hbm.at[pl.ds(part * rows, rows)], out_sems.at[part])
        for part in range(copies_hbm.shape[0] // rows)
    ]
    for store in stores:
        store.start()
    fetches[1].wait()
    low_ref[...] = normed(moving_ref[...])[0].astype(jnp.bfloat16)
    stores.append(pltpu.make_async_copy(low_ref, low_hbm, in_sems.at[2]))
    stores[-1].start()
    for store in stores:
        store.wait()


def pack(*refs):
    rows, width = refs[0].shape
    for k in range(SLOTS):
        refs[-1][k * rows : (k + 1) * rows, :] = refs[k][...]
    refs[-1][SLOTS * rows :, :] = jnp.zeros((PACKED - SLOTS * rows, width), jnp.bfloat16)


def loss_lanes(loss):
    high = loss.astype(jnp.bfloat16).astype(jnp.float32)
    lane = lax.broadcasted_iota(jnp.int32, (loss.shape[0], EXTRA), 1)
    return jnp.where(lane == 0, high, jnp.where(lane == 1, loss - high, 0.0))


def score(
    rows, log_scale_ref, bias_ref, place_ref, text_hbm, own_hbm, other_hbm, grad_hbm, ours_hbm, theirs_hbm,
    text_ref, image_ref, coef_ref, grad_ref, ours_ref, theirs_ref, in_sems, out_sems,
):
    half, width = text_hbm.shape
    piece = half // PIECES
    spans = [pl.ds(part * piece, piece) for part in range(PIECES)]
    image_fetches = [
        pltpu.make_async_copy(image_hbm, image_ref.at[pl.ds(side * PACKED, PACKED)], in_sems.at[side])
        for side, image_hbm in enumerate((own_hbm, other_hbm))
    ]
    text_fetches = [
        pltpu.make_async_copy(text_hbm.at[span], text_ref.at[span], in_sems.at[2 + part])
        for part, span in enumerate(spans)
    ]
    for fetch in image_fetches + text_fetches:
        fetch.start()
    scale = jnp.exp(jnp.full((1, 1), log_scale_ref[0], jnp.float32))
    parity, place = place_ref[0], place_ref[1]
    cols = lax.broadcasted_iota(jnp.int32, (1, PACKED), 1)
    slot = jnp.zeros((1, PACKED), jnp.int32)
    for k in range(1, SLOTS):
        slot = slot + (cols >= k * rows).astype(jnp.int32)
    row_ids = lax.broadcasted_iota(jnp.int32, (piece, PACKED), 0)
    col_ids = lax.broadcasted_iota(jnp.int32, (piece, PACKED), 1)
    for fetch in image_fetches:
        fetch.wait()

    def product(part):
        text_fetches[part].wait()
        return lax.dot_general(
            text_ref[part * piece : (part + 1) * piece, :],
            image_ref[...],
            (((1,), (1,)), ((), ())),
            preferred_element_type=jnp.float32,
        )

    stores = []
    losses = [jnp.zeros((1, PACKED), jnp.float32)] * 2
    ahead = product(0)
    for part, span in enumerate(spans):
        start = part * piece
        block = start // (half // 2)
        offset = 2 * slot + block - parity
        scored = ((offset >= 0) & (offset < STEPS) & (cols < SLOTS * rows)).astype(jnp.float32)
        now = ahead
        if part + 1 < PIECES:
            ahead = product(part + 1)
        for side in range(2):
            here = slice(side * PACKED, (side + 1) * PACKED)
            logit = scale * now[:, here] + bias_ref[0]
            coef = 0.5 * jnp.tanh(0.5 * logit) + 0.5
            term = -jnp.log(1.0 - coef)
            if side == 0:
                positive = (row_ids + start == col_ids + parity * (half // 2) + place) & (col_ids < rows)
                term = term - jnp.where(positive, logit, 0.0)
                coef = coef - jnp.where(positive, 1.0, 0.0)
            losses[side] = losses[side] + scored * jnp.sum(term, axis=0, keepdims=True)
            coef_ref[start : start + piece, here] = (coef * scored).astype(jnp.bfloat16)
        grad_ref[start : start + piece, :] = jnp.dot(
            coef_ref[start : start + piece, :], image_ref[...], preferred_element_type=jnp.float32
        ).astype(jnp.bfloat16)
        stores.append(pltpu.make_async_copy(grad_ref.at[span], grad_hbm.at[span], out_sems.at[part]))
        stores[-1].start()
    for side, (out_ref, out_hbm) in reversed(list(enumerate(((ours_ref, ours_hbm), (theirs_ref, theirs_hbm))))):
        terms = lax.dot_general(
            coef_ref[:, side * PACKED : (side + 1) * PACKED],
            text_ref[...],
            (((0,), (0,)), ((), ())),
            preferred_element_type=jnp.float32,
        )
        loss = jnp.transpose(jnp.broadcast_to(losses[side], (EXTRA, PACKED)))[: SLOTS * rows, :1]
        out_ref[:, :width] = terms[: SLOTS * rows].astype(out_ref.dtype)
        out_ref[:, width:] = loss_lanes(loss).astype(out_ref.dtype)
        stores.append(pltpu.make_async_copy(out_ref, out_hbm, out_sems.at[PIECES + side]))
        stores[-1].start()
    for store in stores:
        store.wait()


def store_sum(out_ref, total):
    width = total.shape[1] - EXTRA
    out_ref[:, :width] = total[:, :width].astype(jnp.bfloat16)
    out_ref[:, width:] = loss_lanes(jnp.sum(total[:, width:], axis=1, keepdims=True)).astype(jnp.bfloat16)


def join(ours_ref, theirs_ref, *grad_refs):
    rows = grad_refs[0].shape[0]
    for k, grad_ref in enumerate(grad_refs):
        here = slice(k * rows, (k + 1) * rows)
        store_sum(grad_ref, ours_ref[here, :] + theirs_ref[here, :].astype(jnp.float32))


def sum_of(refs):
    total = refs[0][...].astype(jnp.float32)
    for ref in refs[1:]:
        total = total + ref[...].astype(jnp.float32)
    return total


def add(*refs):
    store_sum(refs[-1], sum_of(refs[:-1]))


def finish_image(count, log_scale_ref, image_ref, *refs):
    grads, (loss_ref, out_ref) = refs[:-2], refs[-2:]
    width = image_ref.shape[1]
    total = sum_of(grads)
    loss = lax.dot_general(
        jnp.full((8, EXTRA), 1.0 / count, jnp.float32),
        total[:, width:],
        (((1,), (1,)), ((), ())),
        precision=lax.Precision.HIGHEST,
        preferred_element_type=jnp.float32,
    )
    loss_ref[...] = loss[0]
    scale = jnp.exp(jnp.full((1, 1), log_scale_ref[0], jnp.float32))
    unit, norm = normed(image_ref[...])
    out_ref[...] = project(scale * total[:, :width], unit, norm)


def finish_text(log_scale_ref, text_hbm, parts_ref, grad_ref, text_ref, sem):
    fetch = pltpu.make_async_copy(text_hbm, text_ref, sem)
    fetch.start()
    rows = text_ref.shape[0]
    total = parts_ref[:rows, :].astype(jnp.float32)
    for part in range(1, parts_ref.shape[0] // rows):
        total = total + parts_ref[part * rows : (part + 1) * rows, :].astype(jnp.float32)
    scale = jnp.exp(jnp.full((1, 1), log_scale_ref[0], jnp.float32))
    fetch.wait()
    unit, norm = normed(text_ref[...])
    grad_ref[...] = project(scale * total, unit, norm)


def per_device(image, text, log_scale, bias):
    rows, width = image.shape
    plane = lax.axis_size(PLANE)
    half = rows * plane
    smem = pl.BlockSpec(memory_space=pltpu.SMEM)
    vmem = pl.BlockSpec(memory_space=pltpu.VMEM)
    hbm = pl.BlockSpec(memory_space=pltpu.HBM)
    low = jax.ShapeDtypeStruct((rows, width), jnp.bfloat16)
    wide = jax.ShapeDtypeStruct((rows, width + EXTRA), jnp.bfloat16)
    gathered = jax.ShapeDtypeStruct((half, width), jnp.bfloat16)
    full = jax.ShapeDtypeStruct((rows, width), jnp.float32)
    swap = [(0, 1), (1, 0)]
    dma = pltpu.SemaphoreType.DMA

    copies, image_low = call(
        prepare,
        (gathered, low),
        in_specs=[hbm, hbm],
        out_specs=(hbm, hbm),
        scratch_shapes=[pltpu.VMEM((rows, width), jnp.bfloat16)] * 4 + [dma((3,)), dma((plane,))],
        limit=WHOLE,
    )(text, image)
    texts = lax.all_to_all(copies, PLANE, 0, 0, tiled=True)
    one = along_z(image_low, 1)
    two = along_z(image_low, 2)
    three = along_z(two, 1)
    four = along_z(two, 2, (1,))
    own = call(pack, jax.ShapeDtypeStruct((PACKED, width), jnp.bfloat16))(image_low, one, two, three, four)
    other = lax.ppermute(own, "core", swap)

    place = jnp.stack([lax.axis_index("yl"), lax.axis_index(("x", "yh")) * rows]).astype(jnp.int32)
    packed = (SLOTS * rows, width + EXTRA)
    grads, ours, theirs = call(
        functools.partial(score, rows),
        (gathered, jax.ShapeDtypeStruct(packed, jnp.float32), jax.ShapeDtypeStruct(packed, jnp.bfloat16)),
        12 * half * PACKED * width,
        in_specs=[smem] * 3 + [hbm] * 3,
        out_specs=(hbm,) * 3,
        scratch_shapes=[
            pltpu.VMEM((half, width), jnp.bfloat16),
            pltpu.VMEM((2 * PACKED, width), jnp.bfloat16),
            pltpu.VMEM((half, 2 * PACKED), jnp.bfloat16),
            pltpu.VMEM((half, width), jnp.bfloat16),
            pltpu.VMEM(packed, jnp.float32),
            pltpu.VMEM(packed, jnp.bfloat16),
            dma((2 + PIECES,)),
            dma((2 + PIECES,)),
        ],
        limit=WHOLE,
    )(log_scale, bias, place, texts, own, other)
    parts = lax.all_to_all(grads, PLANE, 0, 0, tiled=True)
    terms = call(join, (wide,) * SLOTS)(ours, lax.ppermute(theirs, "core", swap))
    middle = call(add, wide)(terms[2], along_z(terms[3], -1), along_z(terms[4], -2, (1,)))
    back = [terms[0], along_z(terms[1], -1), along_z(middle, -2)]
    loss, grad_image = call(
        functools.partial(finish_image, float(STEPS * half)),
        (jax.ShapeDtypeStruct((rows,), jnp.float32), full),
        in_specs=[smem] + [vmem] * (1 + len(back)),
    )(log_scale, image, *back)
    grad_text = call(
        finish_text,
        full,
        in_specs=[smem, hbm, vmem],
        scratch_shapes=[pltpu.VMEM((rows, width), jnp.bfloat16), dma],
    )(log_scale, text, parts)
    return (loss, grad_image, grad_text)


def solution(mesh):
    axes = ("z", "yl", "x", "yh", "core")
    fine = jax.sharding.Mesh(mesh.devices.reshape(32, 2, 4, 2, 2), axes)
    rows = P(axes, None)
    return jax.shard_map(
        per_device,
        mesh=fine,
        in_specs=(rows, rows, P(), P()),
        out_specs=(P(axes), rows, rows),
        check_vma=False,
    )
```

```python
import functools

import jax
import jax.numpy as jnp
from jax import lax
from jax.experimental import pallas as pl
from jax.experimental.pallas import tpu as pltpu
from jax.sharding import PartitionSpec as P

STEPS = 8
EPS = 1e-06
PLANE = ("yl", "x", "yh")
SLOTS = 5
PACKED = 256
EXTRA = 128
PIECES = 2
LIMIT = 8 * 1024 * 1024
WHOLE = 60 * 1024 * 1024


def call(kernel, out_shape, flops=0, limit=LIMIT, **kwargs):
    return pl.pallas_call(
        kernel,
        out_shape=out_shape,
        compiler_params=pltpu.CompilerParams(vmem_limit_bytes=limit),
        cost_estimate=pl.CostEstimate(flops=flops, bytes_accessed=flops // 512, transcendentals=0) if flops else None,
        **kwargs,
    )


def along_z(value, planes, parities=(0, 1)):
    count = lax.axis_size("z")
    pairs = [(2 * z + yl, 2 * ((z + planes) % count) + yl) for z in range(count) for yl in parities]
    return lax.ppermute(value, ("z", "yl"), pairs)


def normed(rows):
    values = rows.astype(jnp.float32)
    norm = jnp.sqrt(jnp.sum(values * values, axis=-1, keepdims=True) + EPS)
    return (values / norm, norm)


def project(unit_grad, unit, norm):
    inner = jnp.sum(unit * unit_grad, axis=-1, keepdims=True)
    return (unit_grad - unit * inner) / norm


def prepare(still_hbm, moving_hbm, copies_hbm, low_hbm, still_ref, moving_ref, copy_ref, low_ref, in_sems, out_sems):
    fetches = [
        pltpu.make_async_copy(still_hbm, still_ref, in_sems.at[0]),
        pltpu.make_async_copy(moving_hbm, moving_ref, in_sems.at[1]),
    ]
    for fetch in fetches:
        fetch.start()
    fetches[0].wait()
    copy_ref[...] = normed(still_ref[...])[0].astype(jnp.bfloat16)
    rows = copy_ref.shape[0]
    stores = [
        pltpu.make_async_copy(copy_ref, copies_hbm.at[pl.ds(part * rows, rows)], out_sems.at[part])
        for part in range(copies_hbm.shape[0] // rows)
    ]
    for store in stores:
        store.start()
    fetches[1].wait()
    low_ref[...] = normed(moving_ref[...])[0].astype(jnp.bfloat16)
    stores.append(pltpu.make_async_copy(low_ref, low_hbm, in_sems.at[2]))
    stores[-1].start()
    for store in stores:
        store.wait()


def pack(*refs):
    rows, width = refs[0].shape
    for k in range(SLOTS):
        refs[-1][k * rows : (k + 1) * rows, :] = refs[k][...]
    refs[-1][SLOTS * rows :, :] = jnp.zeros((PACKED - SLOTS * rows, width), jnp.bfloat16)


def loss_lanes(loss):
    high = loss.astype(jnp.bfloat16).astype(jnp.float32)
    lane = lax.broadcasted_iota(jnp.int32, (loss.shape[0], EXTRA), 1)
    return jnp.where(lane == 0, high, jnp.where(lane == 1, loss - high, 0.0))


def score(
    rows, scalars_hbm, text_hbm, own_hbm, other_hbm, grad_hbm, ours_hbm, theirs_hbm,
    text_ref, image_ref, coef_ref, grad_ref, ours_ref, theirs_ref, scalars_ref, in_sems, out_sems, scalars_sem,
):
    half, width = text_hbm.shape
    piece = half // PIECES
    spans = [pl.ds(part * piece, piece) for part in range(PIECES)]
    image_fetches = [
        pltpu.make_async_copy(image_hbm, image_ref.at[pl.ds(side * PACKED, PACKED)], in_sems.at[side])
        for side, image_hbm in enumerate((own_hbm, other_hbm))
    ]
    text_fetches = [
        pltpu.make_async_copy(text_hbm.at[span], text_ref.at[span], in_sems.at[2 + part])
        for part, span in enumerate(spans)
    ]
    for fetch in image_fetches + text_fetches:
        fetch.start()
    scalars_fetch = pltpu.make_async_copy(scalars_hbm, scalars_ref, scalars_sem)
    scalars_fetch.start()
    parity, place = lax.axis_index("yl"), lax.axis_index(("x", "yh")) * rows
    cols = lax.broadcasted_iota(jnp.int32, (1, PACKED), 1)
    slot = jnp.zeros((1, PACKED), jnp.int32)
    for k in range(1, SLOTS):
        slot = slot + (cols >= k * rows).astype(jnp.int32)
    row_ids = lax.broadcasted_iota(jnp.int32, (piece, PACKED), 0)
    col_ids = lax.broadcasted_iota(jnp.int32, (piece, PACKED), 1)
    scalars_fetch.wait()
    scale = jnp.exp(scalars_ref[:1, :1])
    bias = scalars_ref[8:9, :1]
    for fetch in image_fetches:
        fetch.wait()

    def product(part):
        text_fetches[part].wait()
        return lax.dot_general(
            text_ref[part * piece : (part + 1) * piece, :],
            image_ref[...],
            (((1,), (1,)), ((), ())),
            preferred_element_type=jnp.float32,
        )

    stores = []
    losses = [jnp.zeros((1, PACKED), jnp.float32)] * 2
    ahead = product(0)
    for part, span in enumerate(spans):
        start = part * piece
        block = start // (half // 2)
        offset = 2 * slot + block - parity
        scored = ((offset >= 0) & (offset < STEPS) & (cols < SLOTS * rows)).astype(jnp.float32)
        now = ahead
        if part + 1 < PIECES:
            ahead = product(part + 1)
        for side in range(2):
            here = slice(side * PACKED, (side + 1) * PACKED)
            logit = scale * now[:, here] + bias
            coef = 0.5 * jnp.tanh(0.5 * logit) + 0.5
            term = -jnp.log(1.0 - coef)
            if side == 0:
                positive = (row_ids + start == col_ids + parity * (half // 2) + place) & (col_ids < rows)
                term = term - jnp.where(positive, logit, 0.0)
                coef = coef - jnp.where(positive, 1.0, 0.0)
            losses[side] = losses[side] + scored * jnp.sum(term, axis=0, keepdims=True)
            coef_ref[start : start + piece, here] = (coef * scored).astype(jnp.bfloat16)
        grad_ref[start : start + piece, :] = jnp.dot(
            coef_ref[start : start + piece, :], image_ref[...], preferred_element_type=jnp.float32
        ).astype(jnp.bfloat16)
        stores.append(pltpu.make_async_copy(grad_ref.at[span], grad_hbm.at[span], out_sems.at[part]))
        stores[-1].start()
    for side, (out_ref, out_hbm) in reversed(list(enumerate(((ours_ref, ours_hbm), (theirs_ref, theirs_hbm))))):
        terms = lax.dot_general(
            coef_ref[:, side * PACKED : (side + 1) * PACKED],
            text_ref[...],
            (((0,), (0,)), ((), ())),
            preferred_element_type=jnp.float32,
        )
        loss = jnp.transpose(jnp.broadcast_to(losses[side], (EXTRA, PACKED)))[: SLOTS * rows, :1]
        out_ref[:, :width] = terms[: SLOTS * rows].astype(out_ref.dtype)
        out_ref[:, width:] = loss_lanes(loss).astype(out_ref.dtype)
        stores.append(pltpu.make_async_copy(out_ref, out_hbm, out_sems.at[PIECES + side]))
        stores[-1].start()
    for store in stores:
        store.wait()


def store_sum(out_ref, total):
    width = total.shape[1] - EXTRA
    out_ref[:, :width] = total[:, :width].astype(jnp.bfloat16)
    out_ref[:, width:] = loss_lanes(jnp.sum(total[:, width:], axis=1, keepdims=True)).astype(jnp.bfloat16)


def join(ours_ref, theirs_ref, *grad_refs):
    rows = grad_refs[0].shape[0]
    for k, grad_ref in enumerate(grad_refs):
        here = slice(k * rows, (k + 1) * rows)
        store_sum(grad_ref, ours_ref[here, :] + theirs_ref[here, :].astype(jnp.float32))


def sum_of(refs):
    total = refs[0][...].astype(jnp.float32)
    for ref in refs[1:]:
        total = total + ref[...].astype(jnp.float32)
    return total


def add(*refs):
    store_sum(refs[-1], sum_of(refs[:-1]))


def finish_image(count, log_scale_ref, image_ref, *refs):
    grads, (loss_ref, out_ref) = refs[:-2], refs[-2:]
    width = image_ref.shape[1]
    total = sum_of(grads)
    loss = lax.dot_general(
        jnp.full((8, EXTRA), 1.0 / count, jnp.float32),
        total[:, width:],
        (((1,), (1,)), ((), ())),
        precision=lax.Precision.HIGHEST,
        preferred_element_type=jnp.float32,
    )
    loss_ref[...] = loss[0]
    scale = jnp.exp(jnp.full((1, 1), log_scale_ref[0], jnp.float32))
    unit, norm = normed(image_ref[...])
    out_ref[...] = project(scale * total[:, :width], unit, norm)


def finish_text(log_scale_ref, text_hbm, parts_ref, grad_ref, text_ref, sem):
    fetch = pltpu.make_async_copy(text_hbm, text_ref, sem)
    fetch.start()
    rows = text_ref.shape[0]
    total = parts_ref[:rows, :].astype(jnp.float32)
    for part in range(1, parts_ref.shape[0] // rows):
        total = total + parts_ref[part * rows : (part + 1) * rows, :].astype(jnp.float32)
    scale = jnp.exp(jnp.full((1, 1), log_scale_ref[0], jnp.float32))
    fetch.wait()
    unit, norm = normed(text_ref[...])
    grad_ref[...] = project(scale * total, unit, norm)


def per_device(image, text, log_scale, bias):
    rows, width = image.shape
    plane = lax.axis_size(PLANE)
    half = rows * plane
    smem = pl.BlockSpec(memory_space=pltpu.SMEM)
    vmem = pl.BlockSpec(memory_space=pltpu.VMEM)
    hbm = pl.BlockSpec(memory_space=pltpu.HBM)
    low = jax.ShapeDtypeStruct((rows, width), jnp.bfloat16)
    wide = jax.ShapeDtypeStruct((rows, width + EXTRA), jnp.bfloat16)
    gathered = jax.ShapeDtypeStruct((half, width), jnp.bfloat16)
    full = jax.ShapeDtypeStruct((rows, width), jnp.float32)
    swap = [(0, 1), (1, 0)]
    dma = pltpu.SemaphoreType.DMA

    copies, image_low = call(
        prepare,
        (gathered, low),
        in_specs=[hbm, hbm],
        out_specs=(hbm, hbm),
        scratch_shapes=[pltpu.VMEM((rows, width), jnp.bfloat16)] * 4 + [dma((3,)), dma((plane,))],
        limit=WHOLE,
    )(text, image)
    texts = lax.all_to_all(copies, PLANE, 0, 0, tiled=True)
    one = along_z(image_low, 1)
    two = along_z(image_low, 2)
    three = along_z(two, 1)
    four = along_z(two, 2, (1,))
    own = call(pack, jax.ShapeDtypeStruct((PACKED, width), jnp.bfloat16))(image_low, one, two, three, four)
    other = lax.ppermute(own, "core", swap)

    scalars = jnp.concatenate([jnp.broadcast_to(value, (8, 128)) for value in (log_scale, bias)])
    packed = (SLOTS * rows, width + EXTRA)
    grads, ours, theirs = call(
        functools.partial(score, rows),
        (gathered, jax.ShapeDtypeStruct(packed, jnp.float32), jax.ShapeDtypeStruct(packed, jnp.bfloat16)),
        12 * half * PACKED * width,
        in_specs=[hbm] * 4,
        out_specs=(hbm,) * 3,
        scratch_shapes=[
            pltpu.VMEM((half, width), jnp.bfloat16),
            pltpu.VMEM((2 * PACKED, width), jnp.bfloat16),
            pltpu.VMEM((half, 2 * PACKED), jnp.bfloat16),
            pltpu.VMEM((half, width), jnp.bfloat16),
            pltpu.VMEM(packed, jnp.float32),
            pltpu.VMEM(packed, jnp.bfloat16),
            pltpu.VMEM((16, 128), jnp.float32),
            dma((2 + PIECES,)),
            dma((2 + PIECES,)),
            dma,
        ],
        limit=WHOLE,
    )(scalars, texts, own, other)
    parts = lax.all_to_all(grads, PLANE, 0, 0, tiled=True)
    terms = call(join, (wide,) * SLOTS)(ours, lax.ppermute(theirs, "core", swap))
    middle = call(add, wide)(terms[2], along_z(terms[3], -1), along_z(terms[4], -2, (1,)))
    back = [terms[0], along_z(terms[1], -1), along_z(middle, -2)]
    loss, grad_image = call(
        functools.partial(finish_image, float(STEPS * half)),
        (jax.ShapeDtypeStruct((rows,), jnp.float32), full),
        in_specs=[smem] + [vmem] * (1 + len(back)),
    )(log_scale, image, *back)
    grad_text = call(
        finish_text,
        full,
        in_specs=[smem, hbm, vmem],
        scratch_shapes=[pltpu.VMEM((rows, width), jnp.bfloat16), dma],
    )(log_scale, text, parts)
    return (loss, grad_image, grad_text)


def solution(mesh):
    axes = ("z", "yl", "x", "yh", "core")
    fine = jax.sharding.Mesh(mesh.devices.reshape(32, 2, 4, 2, 2), axes)
    rows = P(axes, None)
    return jax.shard_map(
        per_device,
        mesh=fine,
        in_specs=(rows, rows, P(), P()),
        out_specs=(P(axes), rows, rows),
        check_vma=False,
    )
```

```python
import functools

import jax
import jax.numpy as jnp
from jax import lax
from jax.experimental import pallas as pl
from jax.experimental.pallas import tpu as pltpu
from jax.sharding import PartitionSpec as P

STEPS = 8
EPS = 1e-06
PLANE = ("yl", "x", "yh")
SLOTS = 5
PACKED = 256
EXTRA = 128
PIECES = 2
LIMIT = 8 * 1024 * 1024
WHOLE = 60 * 1024 * 1024


def call(kernel, out_shape, flops=0, limit=LIMIT, **kwargs):
    return pl.pallas_call(
        kernel,
        out_shape=out_shape,
        compiler_params=pltpu.CompilerParams(vmem_limit_bytes=limit),
        cost_estimate=pl.CostEstimate(flops=flops, bytes_accessed=flops // 512, transcendentals=0) if flops else None,
        **kwargs,
    )


def along_z(value, planes, parities=(0, 1)):
    count = lax.axis_size("z")
    pairs = [(2 * z + yl, 2 * ((z + planes) % count) + yl) for z in range(count) for yl in parities]
    return lax.ppermute(value, ("z", "yl"), pairs)


def normed(rows):
    values = rows.astype(jnp.float32)
    norm = jnp.sqrt(jnp.sum(values * values, axis=-1, keepdims=True) + EPS)
    return (values / norm, norm)


def project(unit_grad, unit, norm):
    inner = jnp.sum(unit * unit_grad, axis=-1, keepdims=True)
    return (unit_grad - unit * inner) / norm


def prepare(still_hbm, moving_hbm, copies_hbm, low_hbm, still_ref, moving_ref, copy_ref, low_ref, in_sems, out_sems):
    fetches = [
        pltpu.make_async_copy(still_hbm, still_ref, in_sems.at[0]),
        pltpu.make_async_copy(moving_hbm, moving_ref, in_sems.at[1]),
    ]
    for fetch in fetches:
        fetch.start()
    fetches[0].wait()
    copy_ref[...] = normed(still_ref[...])[0].astype(jnp.bfloat16)
    rows = copy_ref.shape[0]
    stores = [
        pltpu.make_async_copy(copy_ref, copies_hbm.at[pl.ds(part * rows, rows)], out_sems.at[part])
        for part in range(copies_hbm.shape[0] // rows)
    ]
    for store in stores:
        store.start()
    fetches[1].wait()
    low_ref[...] = normed(moving_ref[...])[0].astype(jnp.bfloat16)
    stores.append(pltpu.make_async_copy(low_ref, low_hbm, in_sems.at[2]))
    stores[-1].start()
    for store in stores:
        store.wait()


def pack(*refs):
    rows, width = refs[0].shape
    for k in range(SLOTS):
        refs[-1][k * rows : (k + 1) * rows, :] = refs[k][...]
    refs[-1][SLOTS * rows :, :] = jnp.zeros((PACKED - SLOTS * rows, width), jnp.bfloat16)


def loss_lanes(loss):
    high = loss.astype(jnp.bfloat16).astype(jnp.float32)
    lane = lax.broadcasted_iota(jnp.int32, (loss.shape[0], EXTRA), 1)
    return jnp.where(lane == 0, high, jnp.where(lane == 1, loss - high, 0.0))


def score(
    rows, scalars_hbm, text_hbm, own_hbm, other_hbm, grad_hbm, ours_hbm, theirs_hbm,
    text_ref, image_ref, coef_ref, grad_ref, ours_ref, theirs_ref, scalars_ref, in_sems, out_sems, scalars_sem,
):
    half, width = text_hbm.shape
    piece = half // PIECES
    spans = [pl.ds(part * piece, piece) for part in range(PIECES)]
    image_fetches = [
        pltpu.make_async_copy(image_hbm, image_ref.at[pl.ds(side * PACKED, PACKED)], in_sems.at[side])
        for side, image_hbm in enumerate((own_hbm, other_hbm))
    ]
    text_fetches = [
        pltpu.make_async_copy(text_hbm.at[span], text_ref.at[span], in_sems.at[2 + part])
        for part, span in enumerate(spans)
    ]
    for fetch in text_fetches[:1] + image_fetches + text_fetches[1:]:
        fetch.start()
    scalars_fetch = pltpu.make_async_copy(scalars_hbm, scalars_ref, scalars_sem)
    scalars_fetch.start()
    parity, place = lax.axis_index("yl"), lax.axis_index(("x", "yh")) * rows
    cols = lax.broadcasted_iota(jnp.int32, (1, PACKED), 1)
    slot = jnp.zeros((1, PACKED), jnp.int32)
    for k in range(1, SLOTS):
        slot = slot + (cols >= k * rows).astype(jnp.int32)
    row_ids = lax.broadcasted_iota(jnp.int32, (piece, PACKED), 0)
    col_ids = lax.broadcasted_iota(jnp.int32, (piece, PACKED), 1)
    scalars_fetch.wait()
    scale = jnp.exp(scalars_ref[:1, :1])
    bias = scalars_ref[8:9, :1]
    for fetch in image_fetches:
        fetch.wait()

    def product(part):
        text_fetches[part].wait()
        return lax.dot_general(
            text_ref[part * piece : (part + 1) * piece, :],
            image_ref[...],
            (((1,), (1,)), ((), ())),
            preferred_element_type=jnp.float32,
        )

    stores = []
    losses = [jnp.zeros((1, PACKED), jnp.float32)] * 2
    ahead = product(0)
    for part, span in enumerate(spans):
        start = part * piece
        block = start // (half // 2)
        offset = 2 * slot + block - parity
        scored = ((offset >= 0) & (offset < STEPS) & (cols < SLOTS * rows)).astype(jnp.float32)
        now = ahead
        if part + 1 < PIECES:
            ahead = product(part + 1)
        for side in range(2):
            here = slice(side * PACKED, (side + 1) * PACKED)
            logit = scale * now[:, here] + bias
            coef = 0.5 * jnp.tanh(0.5 * logit) + 0.5
            term = -jnp.log(1.0 - coef)
            if side == 0:
                positive = (row_ids + start == col_ids + parity * (half // 2) + place) & (col_ids < rows)
                term = term - jnp.where(positive, logit, 0.0)
                coef = coef - jnp.where(positive, 1.0, 0.0)
            losses[side] = losses[side] + scored * jnp.sum(term, axis=0, keepdims=True)
            coef_ref[start : start + piece, here] = (coef * scored).astype(jnp.bfloat16)
        grad_ref[start : start + piece, :] = jnp.dot(
            coef_ref[start : start + piece, :], image_ref[...], preferred_element_type=jnp.float32
        ).astype(jnp.bfloat16)
        stores.append(pltpu.make_async_copy(grad_ref.at[span], grad_hbm.at[span], out_sems.at[part]))
        stores[-1].start()
    for side, (out_ref, out_hbm) in reversed(list(enumerate(((ours_ref, ours_hbm), (theirs_ref, theirs_hbm))))):
        terms = lax.dot_general(
            coef_ref[:, side * PACKED : (side + 1) * PACKED],
            text_ref[...],
            (((0,), (0,)), ((), ())),
            preferred_element_type=jnp.float32,
        )
        loss = jnp.transpose(jnp.broadcast_to(losses[side], (EXTRA, PACKED)))[: SLOTS * rows, :1]
        out_ref[:, :width] = terms[: SLOTS * rows].astype(out_ref.dtype)
        out_ref[:, width:] = loss_lanes(loss).astype(out_ref.dtype)
        stores.append(pltpu.make_async_copy(out_ref, out_hbm, out_sems.at[PIECES + side]))
        stores[-1].start()
    for store in stores:
        store.wait()


def store_sum(out_ref, total):
    width = total.shape[1] - EXTRA
    out_ref[:, :width] = total[:, :width].astype(jnp.bfloat16)
    out_ref[:, width:] = loss_lanes(jnp.sum(total[:, width:], axis=1, keepdims=True)).astype(jnp.bfloat16)


def join(ours_ref, theirs_ref, *grad_refs):
    rows = grad_refs[0].shape[0]
    for k, grad_ref in enumerate(grad_refs):
        here = slice(k * rows, (k + 1) * rows)
        store_sum(grad_ref, ours_ref[here, :].astype(jnp.float32) + theirs_ref[here, :].astype(jnp.float32))


def sum_of(refs):
    total = refs[0][...].astype(jnp.float32)
    for ref in refs[1:]:
        total = total + ref[...].astype(jnp.float32)
    return total


def add(*refs):
    store_sum(refs[-1], sum_of(refs[:-1]))


def finish_image(count, log_scale_ref, image_ref, *refs):
    grads, (loss_ref, out_ref) = refs[:-2], refs[-2:]
    width = image_ref.shape[1]
    total = sum_of(grads)
    loss = lax.dot_general(
        jnp.full((8, EXTRA), 1.0 / count, jnp.float32),
        total[:, width:],
        (((1,), (1,)), ((), ())),
        precision=lax.Precision.HIGHEST,
        preferred_element_type=jnp.float32,
    )
    loss_ref[...] = loss[0]
    scale = jnp.exp(jnp.full((1, 1), log_scale_ref[0], jnp.float32))
    unit, norm = normed(image_ref[...])
    out_ref[...] = project(scale * total[:, :width], unit, norm)


def finish_text(log_scale_ref, text_hbm, parts_ref, grad_ref, text_ref, sem):
    fetch = pltpu.make_async_copy(text_hbm, text_ref, sem)
    fetch.start()
    rows = text_ref.shape[0]
    total = parts_ref[:rows, :].astype(jnp.float32)
    for part in range(1, parts_ref.shape[0] // rows):
        total = total + parts_ref[part * rows : (part + 1) * rows, :].astype(jnp.float32)
    scale = jnp.exp(jnp.full((1, 1), log_scale_ref[0], jnp.float32))
    fetch.wait()
    unit, norm = normed(text_ref[...])
    grad_ref[...] = project(scale * total, unit, norm)


def per_device(image, text, log_scale, bias):
    rows, width = image.shape
    plane = lax.axis_size(PLANE)
    half = rows * plane
    smem = pl.BlockSpec(memory_space=pltpu.SMEM)
    vmem = pl.BlockSpec(memory_space=pltpu.VMEM)
    hbm = pl.BlockSpec(memory_space=pltpu.HBM)
    low = jax.ShapeDtypeStruct((rows, width), jnp.bfloat16)
    wide = jax.ShapeDtypeStruct((rows, width + EXTRA), jnp.bfloat16)
    gathered = jax.ShapeDtypeStruct((half, width), jnp.bfloat16)
    full = jax.ShapeDtypeStruct((rows, width), jnp.float32)
    swap = [(0, 1), (1, 0)]
    dma = pltpu.SemaphoreType.DMA

    copies, image_low = call(
        prepare,
        (gathered, low),
        in_specs=[hbm, hbm],
        out_specs=(hbm, hbm),
        scratch_shapes=[pltpu.VMEM((rows, width), jnp.bfloat16)] * 4 + [dma((3,)), dma((plane,))],
        limit=WHOLE,
    )(text, image)
    texts = lax.all_to_all(copies, PLANE, 0, 0, tiled=True)
    one = along_z(image_low, 1)
    two = along_z(image_low, 2)
    three = along_z(two, 1)
    four = along_z(two, 2, (1,))
    own = call(pack, jax.ShapeDtypeStruct((PACKED, width), jnp.bfloat16))(image_low, one, two, three, four)
    other = lax.ppermute(own, "core", swap)

    scalars = jnp.concatenate([jnp.broadcast_to(value, (8, 128)) for value in (log_scale, bias)])
    packed = (SLOTS * rows, width + EXTRA)
    grads, ours, theirs = call(
        functools.partial(score, rows),
        (gathered, jax.ShapeDtypeStruct(packed, jnp.bfloat16), jax.ShapeDtypeStruct(packed, jnp.bfloat16)),
        12 * half * PACKED * width,
        in_specs=[hbm] * 4,
        out_specs=(hbm,) * 3,
        scratch_shapes=[
            pltpu.VMEM((half, width), jnp.bfloat16),
            pltpu.VMEM((2 * PACKED, width), jnp.bfloat16),
            pltpu.VMEM((half, 2 * PACKED), jnp.bfloat16),
            pltpu.VMEM((half, width), jnp.bfloat16),
            pltpu.VMEM(packed, jnp.bfloat16),
            pltpu.VMEM(packed, jnp.bfloat16),
            pltpu.VMEM((16, 128), jnp.float32),
            dma((2 + PIECES,)),
            dma((2 + PIECES,)),
            dma,
        ],
        limit=WHOLE,
    )(scalars, texts, own, other)
    parts = lax.all_to_all(grads, PLANE, 0, 0, tiled=True)
    terms = call(join, (wide,) * SLOTS)(ours, lax.ppermute(theirs, "core", swap))
    middle = call(add, wide)(terms[2], along_z(terms[3], -1), along_z(terms[4], -2, (1,)))
    back = [terms[0], along_z(terms[1], -1), along_z(middle, -2)]
    loss, grad_image = call(
        functools.partial(finish_image, float(STEPS * half)),
        (jax.ShapeDtypeStruct((rows,), jnp.float32), full),
        in_specs=[smem] + [vmem] * (1 + len(back)),
    )(log_scale, image, *back)
    grad_text = call(
        finish_text,
        full,
        in_specs=[smem, hbm, vmem],
        scratch_shapes=[pltpu.VMEM((rows, width), jnp.bfloat16), dma],
    )(log_scale, text, parts)
    return (loss, grad_image, grad_text)


def solution(mesh):
    axes = ("z", "yl", "x", "yh", "core")
    fine = jax.sharding.Mesh(mesh.devices.reshape(32, 2, 4, 2, 2), axes)
    rows = P(axes, None)
    return jax.shard_map(
        per_device,
        mesh=fine,
        in_specs=(rows, rows, P(), P()),
        out_specs=(P(axes), rows, rows),
        check_vma=False,
    )
```
